256 devices in a mesh: section: 4 (over x), dp: 8 (over z), mp: 8 (over y, core).
Axes of the slice: x: 4, y: 4, z: 8, core: 2. Of those that a mesh axis runs over, the one named last changes fastest.
Arguments:
- query_inputs: bfloat16 [1024, 4096], P('dp', 'mp'), may hold values from -12 to 12
- section_weights: bfloat16 [16384, 4096], P('section', 'mp'), may hold values from -0.09375 to 0.09375
- head_weight: bfloat16 [4096, 4096], P(None, 'mp'), may hold values from -0.09375 to 0.09375
- passages: bfloat16 [4096, 4096], P(('section', 'dp', 'mp')), may hold values from -32 to 32
- query_cells: int32 [1024], P('dp'), may hold values from 0 to 15
- passage_cells: int32 [4096], P(('section', 'dp', 'mp')), may hold values from 0 to 15
- positives: int32 [1024], P('dp'), may hold values from 0 to 4095
- master: float32 [4096, 4096], P(('section', 'dp'), 'mp'), may hold values from -0.09375 to 0.09375
- moment_one: float32 [4096, 4096], P(('section', 'dp'), 'mp'), may hold values from -3 to 3
- moment_two: float32 [4096, 4096], P(('section', 'dp'), 'mp'), may hold values from 0.1 to 10
Outputs:
- loss: float32 [1024], P('dp')
- passage_grads: float32 [4096, 4096], P(('section', 'dp', 'mp'))
- new_master: float32 [4096, 4096], P(('section', 'dp'), 'mp')
- new_moment_one: float32 [4096, 4096], P(('section', 'dp'), 'mp')
- new_moment_two: float32 [4096, 4096], P(('section', 'dp'), 'mp')
The draws below stay inside these ranges and needn't reach their ends.
Inputs may be any that keep to these rules, and one draw needn't show every extreme that they name: `query_cells`: cell ids. `passage_cells`: cell ids. `positives`: passage indices.
All inputs are finite; a program needn't handle non-finite values.
Results may differ from the reference program's by a relative error of at most 0.0095.
Values may be sent and summed in bfloat16 or wider, within the bound.
No kernel may reach another device: no remote copies, remote signals or barrier semaphores. Data moves between devices by JAX's collectives and lax.ppermute only.
A program may use at most 64 MiB of HBM per device.

```python
import math
import jax
import jax.numpy as jnp
import numpy as np
from jax import lax

D = 4096
PB = 16
CELLS = 16
NQ = 1024
NP = 4096
N_SECTION = 4
N_DP = 8
N_MP = 8


def common_sign(key):
    return jnp.where(jax.random.bernoulli(key, 0.5, (D,)), 1.0, -1.0).astype(jnp.float32)


def draw_query_inputs(key, part):
    shared = common_sign(key)
    key = jax.random.fold_in(key, 11)
    first, second = jax.random.split(key)
    base = jnp.clip(jax.random.normal(first, (NQ, D), jnp.float32), -6.0, 6.0)
    amount = 2.0
    chosen = jax.random.bernoulli(second, 1.0 / 16.0, (NQ, 1)).astype(jnp.float32)
    values = base + chosen * amount * shared[None, :]
    return jnp.clip(values, -12.0, 12.0).astype(jnp.bfloat16)


def draw_passages(key, part):
    shared = common_sign(key)
    key = jax.random.fold_in(key, 23)
    first, second, third = jax.random.split(key, 3)
    base = jnp.clip(jax.random.normal(first, (NP, D), jnp.float32), -6.0, 6.0)
    strength = jax.random.uniform(third, (NP, 1), jnp.float32, 100.0, 400.0) / (2.0 * D ** 0.5)
    chosen = jax.random.bernoulli(second, 1.0 / 32.0, (NP, 1)).astype(jnp.float32)
    values = base + chosen * strength * shared[None, :]
    return jnp.clip(values, -32.0, 32.0).astype(jnp.bfloat16)


def place_ends(values, stream_key, smallest, top_value):
    longest = values.shape.index(max(values.shape))
    spots = []
    for shift in (0, 1):
        where = [jax.random.randint(jax.random.fold_in(stream_key, axis), (), 0, length) for axis, length in enumerate(values.shape)]
        where[longest] = (where[longest] + shift) % values.shape[longest]
        spots.append(tuple(where))
    return values.at[spots[0]].set(smallest).at[spots[1]].set(top_value)


def level_of(stream_key, shape, cuts, least, largest):
    loudness, own = 1.0, jax.random.fold_in(stream_key, 6)
    for position, blocks in cuts:
        draws = jnp.exp(jax.random.uniform(jax.random.fold_in(own, position), (blocks,), jnp.float32, least / len(cuts), largest / len(cuts)))
        loudness = loudness * jnp.repeat(draws, shape[position] // blocks).reshape([-1 if axis == position else 1 for axis in range(len(shape))])
    return loudness


def cumulative_ranks(number_of, skew):
    weights = [(1 << 20) // math.isqrt(grade ** skew) + 1 for grade in range(1, number_of + 1)]
    spread = 1 + sum(weights) // (1 << 30)
    return np.cumsum(np.array([max(1, weight // spread) for weight in weights]))


def ranked(own_key, dims, count, lean):
    table = cumulative_ranks(count, lean)
    pick = jax.random.randint(jax.random.fold_in(own_key, 1), dims, 0, int(table[count - 1]))
    grade = jnp.searchsorted(jnp.asarray(table, jnp.int32), pick, side="right")
    return jax.random.permutation(jax.random.fold_in(own_key, 2), count)[grade].astype(jnp.int32)


def scatter_about(own_key, extent, deviation, most, cuts=(), kind=jnp.bfloat16):
    level = level_of(own_key, extent, cuts, -0.22, 0.18) if cuts else 1.0
    entries = jax.random.normal(own_key, extent, jnp.float32) * deviation * level
    return jnp.minimum(jnp.maximum(entries, -most), most).astype(kind)


def setup_inputs(seed: int = 0) -> dict:
    keys = jax.random.split(jax.random.key(seed), 11)
    query_inputs = draw_query_inputs(jax.random.fold_in(keys[10], 71), 0)
    section_weights = scatter_about(keys[1], (N_SECTION * D, D), D ** -0.5, 0.09375, ((0, 4), (1, 8)))
    head_weight = scatter_about(keys[2], (D, D), D ** -0.5, 0.09375, ((1, 8),))
    passages = draw_passages(jax.random.fold_in(keys[10], 71), 0)
    query_cells = place_ends(ranked(keys[4], (NQ,), CELLS, 2), jax.random.fold_in(keys[4], 3), 0, CELLS - 1).astype(jnp.int32)
    passage_cells = place_ends(ranked(keys[5], (NP,), CELLS, 2), jax.random.fold_in(keys[5], 3), 0, CELLS - 1).astype(jnp.int32)
    positives = place_ends(jax.random.randint(keys[6], (NQ,), 0, NP), jax.random.fold_in(keys[6], 1), 0, NP - 1).astype(jnp.int32)
    master = scatter_about(keys[7], (D, D), D ** -0.5, 0.09375, ((0, 32), (1, 8)), jnp.float32)
    moment_one = scatter_about(keys[8], (D, D), 0.5, 3.0, ((0, 32), (1, 8)), jnp.float32)
    moment_two = jnp.clip(jnp.exp(math.log(10.0) - 4.6051702 * jax.random.uniform(keys[9], (D, D), jnp.float32) ** level_of(keys[9], (D, D), ((0, 32), (1, 8)), -0.2, 0.2)), 0.1, 10.0)
    return {"query_inputs": query_inputs, "section_weights": section_weights, "head_weight": head_weight, "passages": passages, "query_cells": query_cells, "passage_cells": passage_cells, "positives": positives, "master": master, "moment_one": moment_one, "moment_two": moment_two}


correct_one = 0.9999734386011124
correct_two = 0.994079470779666

def rms_rows(values):
    wide = values.astype(jnp.float32)
    return (wide * lax.rsqrt(lax.optimization_barrier(jnp.mean(wide * wide, axis=1, keepdims=True)) + 1e-06)).astype(jnp.bfloat16)

def silu_slope(values):
    sig = jax.nn.sigmoid(values)
    return sig * (1.0 + values * (1.0 - sig))

def reference(query_inputs, section_weights, head_weight, passages, query_cells, passage_cells, positives, master, moment_one, moment_two):
    hidden = query_inputs
    for layer_at in range(N_SECTION):
        weight = section_weights[layer_at * D:(layer_at + 1) * D]
        mixed = jnp.dot(rms_rows(hidden), weight, preferred_element_type=jnp.float32)
        hidden = (hidden.astype(jnp.float32) + jax.nn.silu(mixed)).astype(jnp.bfloat16)
    normed = rms_rows(hidden)
    head = jnp.dot(normed, head_weight, preferred_element_type=jnp.float32)
    query_emb = (hidden.astype(jnp.float32) + jax.nn.silu(head)).astype(jnp.bfloat16)
    scale = D ** (-0.5)
    count = N_SECTION * N_MP
    group_rows = N_DP * PB

    def regroup(values):
        shape = values.shape[1:]
        shaped = values.reshape((N_SECTION, N_DP, N_MP, PB) + shape)
        shaped = jnp.swapaxes(shaped, 1, 2)
        return shaped.reshape((count, group_rows) + shape)
    groups = regroup(passages)
    cells = regroup(passage_cells)
    indices = regroup(jnp.arange(NP, dtype=jnp.int32))

    def scores_of(group, cell, index):
        score = jnp.dot(group, query_emb.T, preferred_element_type=jnp.float32) * scale
        hit = index[:, None] == positives[None, :]
        allowed = jnp.logical_or(hit, cell[:, None] == query_cells[None, :])
        return (score, allowed, hit)

    def first_pass(carry, item):
        top, total, positive = carry
        score, allowed, hit = scores_of(*item)
        masked = jnp.where(allowed, score, -1e+30)
        newtop = jnp.maximum(top, lax.optimization_barrier(jnp.max(masked, axis=0)))
        total = total * jnp.exp(top - newtop) + lax.optimization_barrier(jnp.sum(jnp.exp(masked - newtop[None, :]), axis=0))
        positive = positive + lax.optimization_barrier(jnp.sum(jnp.where(hit, score, 0.0), axis=0))
        return ((newtop, total, positive), None)
    start = (jnp.full((NQ,), -1e+30, jnp.float32), jnp.zeros((NQ,), jnp.float32), jnp.zeros((NQ,), jnp.float32))
    (top, total, positive), unused = lax.scan(first_pass, start, (groups, cells, indices))
    lse = top + jnp.log(total)
    loss = lse - positive

    def second_pass(query_grad, item):
        group, cell, index = item
        score, allowed, hit = scores_of(group, cell, index)
        masked = jnp.where(allowed, score, -1e+30)
        prob = (jnp.exp(masked - lse[None, :]) - jnp.where(hit, 1.0, 0.0)).astype(jnp.bfloat16)
        part = (jnp.dot(prob.T, group, preferred_element_type=jnp.float32) * scale).astype(jnp.bfloat16)
        query_grad = query_grad + lax.optimization_barrier(part).astype(jnp.float32)
        passage_part = jnp.dot(prob, query_emb, preferred_element_type=jnp.float32) * scale
        return (query_grad, passage_part)
    slope = silu_slope(head)
    weight_grad = jnp.zeros((D, D), jnp.float32)
    passage_parts = []
    for section_at in range(N_SECTION):
        lo = section_at * N_MP
        hi = lo + N_MP
        query_grad, passage_part = lax.scan(second_pass, jnp.zeros((NQ, D), jnp.float32), (groups[lo:hi], cells[lo:hi], indices[lo:hi]))
        head_grad = (query_grad * slope).astype(jnp.bfloat16)
        weight_grad = weight_grad + jnp.dot(normed.T, head_grad, preferred_element_type=jnp.float32)
        passage_parts.append(passage_part)
    stacked = jnp.stack(passage_parts).reshape(N_SECTION, N_MP, N_DP, PB, D)
    passage_grads = jnp.swapaxes(stacked, 1, 2).reshape(NP, D)
    new_moment_one = 0.9 * moment_one + 0.1 * weight_grad
    new_moment_two = 0.95 * moment_two + 0.05 * weight_grad * weight_grad
    update = new_moment_one / correct_one / (jnp.sqrt(new_moment_two / correct_two) + 1e-08)
    new_master = master - 0.001 * (update + 0.1 * master)
    return (loss, passage_grads, new_master, new_moment_one, new_moment_two)
```

```python
import functools
import math

import jax
import jax.numpy as jnp
from jax import lax
from jax.experimental import pallas as pl
from jax.experimental.pallas import tpu as pltpu
from jax.sharding import Mesh, PartitionSpec as P

correct_one = 0.9999734386011124
correct_two = 0.994079470779666
FAR = -1e30
F32 = jnp.float32
BF16 = jnp.bfloat16
VMEM = pl.BlockSpec(memory_space=pltpu.VMEM)
SMEM = pl.BlockSpec(memory_space=pltpu.SMEM)
PARAMS = pltpu.CompilerParams(vmem_limit_bytes=48 * 1024 * 1024)


def turned(block, axis, steps):
    count = lax.axis_size(axis)
    return lax.ppermute(block, axis, [(i, (i + steps) % count) for i in range(count)])


def spread(block):
    count = lax.axis_size("y")
    near = jnp.stack([block] + [turned(block, "y", k) for k in range(1, count)])
    return near, turned(near, "core", 1)


def silu(u):
    return u * jax.nn.sigmoid(u)


def row_scale(near, far):
    square = 0.0
    for ref in (near, far):
        for k in range(ref.shape[0]):
            wide = ref[k].astype(F32)
            square = square + jnp.sum(wide * wide, axis=1, keepdims=True)
    width = 2 * near.shape[0] * near.shape[2]
    return lax.rsqrt(square / width + 1e-06)


def owners(place, near, far):
    count = near.shape[0]
    y, core = place[2], place[3]
    for k in range(count):
        for ref, c in ((near, core), (far, 1 - core)):
            yield ref, k, lax.rem(y - k + count, count) * 2 + c


def mixed_rows(place, near, far, weight, normed=None):
    scale = row_scale(near, far)
    wide = near.shape[2]
    total = 0.0
    for ref, k, owner in owners(place, near, far):
        rows = (ref[k].astype(F32) * scale).astype(BF16)
        at = pl.ds(pl.multiple_of(owner * wide, wide), wide)
        if normed is not None:
            normed[:, at] = rows
        total = total + jnp.dot(rows, weight[at, :], preferred_element_type=F32)
    return total


def layer_kernel(place, near, far, weight, out):
    mixed = mixed_rows(place, near, far, weight)
    out[...] = (near[0].astype(F32) + silu(mixed)).astype(BF16)


def head_kernel(place, near, far, weight, emb, slope, normed):
    head = mixed_rows(place, near, far, weight, normed)
    sig = jax.nn.sigmoid(head)
    emb[...] = (near[0].astype(F32) + head * sig).astype(BF16)
    slope[...] = sig * (1.0 + head * (1.0 - sig))


def masks(place, passages, query_cells, positives, sizes):
    width, cycle, parts, block = sizes
    rows, queries = passages.shape[0], positives.shape[1]
    at = lax.broadcasted_iota(jnp.int32, (rows, queries), 0)
    owner, inner = at // block, at % block
    part = place[2] * 2 + place[3]
    index = ((place[0] * cycle + owner) * parts + part) * block + inner
    hit = index == positives[...]
    cells = passages[:, width : width + queries].astype(F32)
    allowed = jnp.logical_or(hit, cells == query_cells[...].astype(F32))
    return hit, allowed


def score_kernel(sizes, place, near, far, passages, query_cells, positives, score, stats, full):
    wide = near.shape[2]
    total = 0.0
    for ref, k, owner in owners(place, near, far):
        at = pl.ds(pl.multiple_of(owner * wide, wide), wide)
        full[:, at] = ref[k]
        total = total + lax.dot_general(
            passages[:, at], ref[k], (((1,), (1,)), ((), ())), preferred_element_type=F32
        )
    total = total * sizes[0] ** -0.5
    score[...] = total
    hit, allowed = masks(place, passages, query_cells, positives, sizes)
    masked = jnp.where(allowed, total, FAR)
    top = jnp.max(masked, axis=0, keepdims=True)
    summed = jnp.sum(jnp.exp(masked - top), axis=0, keepdims=True)
    positive = jnp.sum(jnp.where(hit, total, 0.0), axis=0, keepdims=True)
    rest = jnp.zeros((5,) + top.shape[1:], F32)
    packed = jnp.concatenate([top, summed, positive, rest], axis=0)
    stats[...] = jnp.broadcast_to(packed[None], stats.shape)


def grad_kernel(
    sizes, place, stats, score, full, passages, query_cells, positives, loss, send, keep, grads
):
    width = sizes[0]
    top, summed, positive = stats[:, 0, :], stats[:, 1, :], stats[:, 2, :]
    upper = jnp.max(top, axis=0, keepdims=True)
    total = jnp.sum(summed * jnp.exp(top - upper), axis=0, keepdims=True)
    lse = upper + jnp.log(total)
    loss[...] = lse - jnp.sum(positive, axis=0, keepdims=True)
    hit, allowed = masks(place, passages, query_cells, positives, sizes)
    masked = jnp.where(allowed, score[...], FAR)
    prob = jnp.exp(masked - lse) - jnp.where(hit, 1.0, 0.0)
    turned_prob = prob.T.astype(BF16)
    prob = prob.astype(BF16)
    factor = width**-0.5
    sections, count, rows, wide = keep.shape
    core = place[3]
    for j in range(count):
        for ref, c in ((keep, core), (send, 1 - core)):
            at = pl.ds(pl.multiple_of((2 * j + c) * wide, wide), wide)
            part = jnp.dot(turned_prob, passages[:, at], preferred_element_type=F32) * factor
            part = part.astype(BF16)
            for s in range(sections):
                ref[s, j] = part[s * rows : (s + 1) * rows]
    for j in range(0, width, wide):
        part = jnp.dot(prob, full[:, j : j + wide], preferred_element_type=F32) * factor
        part = part.astype(BF16)
        cycle, block = grads.shape[:2]
        for d in range(cycle):
            grads[d, :, j : j + wide] = part[d * block : (d + 1) * block]


def call(kernel, outs, *args):
    return pl.pallas_call(
        kernel,
        out_shape=[jax.ShapeDtypeStruct(shape, dtype) for shape, dtype in outs],
        in_specs=[SMEM] + [VMEM] * (len(args) - 1),
        out_specs=[VMEM] * len(outs),
        compiler_params=PARAMS,
    )(*args)


def shards(
    query_inputs,
    section_weights,
    head_weight,
    passages,
    query_cells,
    passage_cells,
    positives,
    master,
    moment_one,
    moment_two,
):
    sections = lax.axis_size("section")
    cycle = lax.axis_size("dp")
    count = lax.axis_size("y")
    section_at = lax.axis_index("section")
    place = jnp.stack(
        [section_at, lax.axis_index("dp"), lax.axis_index("y"), lax.axis_index("core")]
    ).astype(jnp.int32)
    queries, wide = query_inputs.shape
    block, width = passages.shape
    sizes = (width, cycle, 2 * count, block)
    with jax.named_scope("passages"):
        cells = jnp.broadcast_to(passage_cells.astype(BF16)[:, None], (block, queries))
        held = lax.all_gather(
            jnp.concatenate([passages, cells], axis=1), "dp", axis=0, tiled=True
        )
    local = query_inputs
    for layer in range(sections):
        with jax.named_scope("tower"):
            near, far = spread(local)
            (local,) = call(
                layer_kernel, [((queries, wide), BF16)], place, near, far, section_weights
            )
            if layer + 1 < sections:
                local = turned(local, "section", 1)
    with jax.named_scope("to_sections"):
        last = sections - 1
        final = jnp.where(section_at == last, local, 0).astype(BF16)
        for other in range(last):
            final = final + lax.ppermute(local, "section", [(last, other)])
    with jax.named_scope("head"):
        near, far = spread(final)
        query_cols, slope, normed = call(
            head_kernel,
            [((queries, wide), BF16), ((queries, wide), F32), ((queries, width), BF16)],
            place, near, far, head_weight,
        )
    rows = queries // sections
    with jax.named_scope("normed_home"):
        mine = lax.dynamic_slice_in_dim(normed, section_at * rows, rows, 0)
        mine = mine.reshape(rows, sections, cycle, width // (sections * cycle))
        mine = mine.transpose(2, 0, 1, 3).reshape(cycle, rows, width // cycle)
        normed_all = lax.all_to_all(mine, "dp", 0, 0).reshape(cycle * rows, width // cycle)
    with jax.named_scope("score"):
        near, far = spread(query_cols)
        row_cells, row_positives = query_cells[None, :], positives[None, :]
        group = sections * count * 2
        score, stats, full = call(
            functools.partial(score_kernel, sizes),
            [
                ((cycle * block, queries), F32),
                ((group, 8, queries), F32),
                ((queries, width), BF16),
            ],
            place, near, far, held, row_cells, row_positives,
        )
    with jax.named_scope("stats"):
        stats = lax.all_to_all(stats, ("section", "y", "core"), 0, 0)
    with jax.named_scope("grad"):
        half = (sections, count, rows, wide)
        loss, send, keep, grads = call(
            functools.partial(grad_kernel, sizes),
            [((1, queries), F32), (half, BF16), (half, BF16), ((cycle, block, width), BF16)],
            place, stats, score, full, held, row_cells, row_positives,
        )
    with jax.named_scope("passage_grads"):
        grads = lax.all_to_all(grads, "dp", 0, 0)
        passage_grads = jnp.sum(grads.astype(F32), axis=0)
    with jax.named_scope("query_grad"):
        keep = (keep.astype(F32) + turned(send, "core", 1).astype(F32)).astype(BF16)
        parts = lax.all_to_all(keep.reshape(sections * count, rows, wide), ("section", "y"), 0, 0)
        query_grad = jnp.sum(parts.astype(F32), axis=0)
        head_grad = query_grad * lax.dynamic_slice_in_dim(slope, section_at * rows, rows, 0)
        head_grad = jnp.broadcast_to(head_grad.astype(BF16)[None], (cycle, rows, wide))
        head_grad = lax.all_to_all(head_grad, "dp", 0, 0).reshape(cycle * rows, wide)
    with jax.named_scope("weight_grad"):
        part = jnp.einsum("qd,qc->dc", normed_all, head_grad, preferred_element_type=F32)
        part = part.astype(BF16).reshape(sections, width // (sections * cycle), wide)
        part = lax.all_to_all(part, "section", 0, 0)
        weight_grad = jnp.sum(part.astype(F32), axis=0)
    new_moment_one = 0.9 * moment_one + 0.1 * weight_grad
    new_moment_two = 0.95 * moment_two + 0.05 * weight_grad * weight_grad
    update = new_moment_one / correct_one / (jnp.sqrt(new_moment_two / correct_two) + 1e-08)
    new_master = master - 0.001 * (update + 0.1 * master)
    return (loss[0], passage_grads, new_master, new_moment_one, new_moment_two)


def solution(mesh):
    sections, cycle, parts = (mesh.shape[axis] for axis in ("section", "dp", "mp"))
    split = Mesh(
        mesh.devices.reshape(sections, cycle, parts // 2, 2), ("section", "dp", "y", "core")
    )
    mp = ("y", "core")
    everything = ("section", "dp") + mp
    tile = P(("section", "dp"), mp)
    return jax.shard_map(
        shards,
        mesh=split,
        in_specs=(
            P("dp", mp),
            P("section", mp),
            P(None, mp),
            P(everything, None),
            P("dp"),
            P(everything),
            P("dp"),
            tile,
            tile,
            tile,
        ),
        out_specs=(P("dp"), P(everything, None), tile, tile, tile),
        check_vma=False,
    )
```

```python
import functools

import jax
import jax.numpy as jnp
from jax import lax
from jax.experimental import pallas as pl
from jax.experimental.pallas import tpu as pltpu
from jax.sharding import Mesh, PartitionSpec as P

correct_one = 0.9999734386011124
correct_two = 0.994079470779666
FAR = -1e30
F32 = jnp.float32
BF16 = jnp.bfloat16
VMEM = pl.BlockSpec(memory_space=pltpu.VMEM)
SMEM = pl.BlockSpec(memory_space=pltpu.SMEM)
LOOSE = pl.BlockSpec(memory_space=pltpu.HBM)
COST = pl.CostEstimate(flops=1024, bytes_accessed=1024, transcendentals=0)
PARAMS = pltpu.CompilerParams(vmem_limit_bytes=16 * 1024 * 1024)


def turned(block, axis, steps):
    count = lax.axis_size(axis)
    return lax.ppermute(block, axis, [(i, (i + steps) % count) for i in range(count)])


def spread(block):
    count = lax.axis_size("y")
    near = jnp.stack([block] + [turned(block, "y", k) for k in range(1, count)])
    return near, turned(near, "core", 1)


def stack_kernel(place, *rest):
    out = rest[-1]
    for k in range(out.shape[0]):
        out[k] = rest[k][...]


def spread_after(block, place, loose):
    if not loose:
        return spread(block)
    count = lax.axis_size("y")
    blocks = [block] + [turned(block, "y", k) for k in range(1, count)]
    (near,) = call(stack_kernel, [((count,) + block.shape, block.dtype)], [place] + blocks, loose)
    return near, turned(near, "core", 1)


def silu(u):
    return u * jax.nn.sigmoid(u)


def row_scale(near, far):
    square = 0.0
    for ref in (near, far):
        for k in range(ref.shape[0]):
            wide = ref[k].astype(F32)
            square = square + jnp.sum(wide * wide, axis=1, keepdims=True)
    width = 2 * near.shape[0] * near.shape[2]
    return lax.rsqrt(square / width + 1e-06)


def owners(place, near, far):
    count = near.shape[0]
    y, core = place[2], place[3]
    for k in range(count):
        for ref, c in ((near, core), (far, 1 - core)):
            yield ref, k, lax.rem(y - k + count, count) * 2 + c


def at_block(owner, wide):
    return pl.ds(pl.multiple_of(owner * wide, wide), wide)


def mixed_rows(place, near, far, weight, normed=None):
    scale = row_scale(near, far)
    wide = near.shape[2]
    total = 0.0
    for ref, k, owner in owners(place, near, far):
        rows = (ref[k].astype(F32) * scale).astype(BF16)
        at = at_block(owner, wide)
        if normed is not None:
            normed[:, at] = rows
        total = total + jnp.dot(rows, weight[at, :], preferred_element_type=F32)
    return total


def load_kernel(place, source, *rest):
    out, sem = rest[-2:]
    copy = pltpu.make_async_copy(source, out, sem)
    copy.start()
    copy.wait()


def loaded(place, weight, after):
    (out,) = call(
        load_kernel,
        [(weight.shape, weight.dtype)],
        [place, weight],
        after,
        scratch=[pltpu.SemaphoreType.DMA],
        far_off=(1,),
    )
    return out


def layer_kernel(place, near, far, weight, *rest):
    out = rest[-1]
    mixed = mixed_rows(place, near, far, weight)
    out[...] = (near[0].astype(F32) + silu(mixed)).astype(BF16)


def head_kernel(place, near, far, weight, emb, slope, pieces, normed):
    head = mixed_rows(place, near, far, weight, normed)
    sig = jax.nn.sigmoid(head)
    emb[...] = (near[0].astype(F32) + head * sig).astype(BF16)
    slope[...] = sig * (1.0 + head * (1.0 - sig))
    cycle, rows, taken = pieces.shape
    sections = normed.shape[0] // rows
    piece = taken // sections
    own = pl.ds(pl.multiple_of(place[0] * rows, rows), rows)
    for k in range(cycle):
        for s in range(sections):
            at = (s * cycle + k) * piece
            pieces[k, :, s * piece : (s + 1) * piece] = normed[own, at : at + piece]


def head_grad_kernel(place, parts, slope, *rest):
    out = rest[-1]
    cycle, rows, wide = out.shape
    total = 0.0
    for k in range(parts.shape[0]):
        total = total + parts[k].astype(F32)
    own = pl.ds(pl.multiple_of(place[0] * rows, rows), rows)
    grad = (total * slope[own, :]).astype(BF16)
    for k in range(cycle):
        out[k] = grad


def weight_grad_kernel(place, grads, pieces, out):
    cycle, rows, wide = grads.shape
    taken = out.shape[1]
    part = lax.dot_general(
        pieces[...].reshape(cycle * rows, pieces.shape[2]),
        grads[...].reshape(cycle * rows, wide),
        (((0,), (0,)), ((), ())),
        preferred_element_type=F32,
    ).astype(BF16)
    for s in range(out.shape[0]):
        out[s] = part[s * taken : (s + 1) * taken]


def update_kernel(
    place, parts, master, moment_one, moment_two, grads, new_master, new_one, new_two, new_grads
):
    grad = 0.0
    for k in range(parts.shape[0]):
        grad = grad + parts[k].astype(F32)
    one = 0.9 * moment_one[...] + 0.1 * grad
    two = 0.95 * moment_two[...] + 0.05 * grad * grad
    update = one / correct_one / (jnp.sqrt(two / correct_two) + 1e-08)
    new_master[...] = master[...] - 0.001 * (update + 0.1 * master[...])
    new_one[...] = one
    new_two[...] = two
    new_grads[...] = grads[...].astype(F32)


def masks(place, passages, query_cells, positives, sizes):
    width, cycle, parts, block = sizes
    rows, queries = passages.shape[0], positives.shape[1]
    at = lax.broadcasted_iota(jnp.int32, (rows, queries), 0)
    owner, inner = at // block, at % block
    part = place[2] * 2 + place[3]
    index = ((place[0] * cycle + owner) * parts + part) * block + inner
    hit = index == positives[...]
    cells = passages[:, width : width + queries].astype(F32)
    allowed = jnp.logical_or(hit, cells == query_cells[...].astype(F32))
    return hit, allowed


def score_kernel(sizes, place, near, far, passages, query_cells, positives, score, stats, full):
    wide = near.shape[2]
    total = 0.0
    for ref, k, owner in owners(place, near, far):
        at = pl.ds(pl.multiple_of(owner * wide, wide), wide)
        full[:, at] = ref[k]
        total = total + lax.dot_general(
            passages[:, at], ref[k], (((1,), (1,)), ((), ())), preferred_element_type=F32
        )
    total = total * sizes[0] ** -0.5
    score[...] = total
    hit, allowed = masks(place, passages, query_cells, positives, sizes)
    masked = jnp.where(allowed, total, FAR)
    top = jnp.max(masked, axis=0, keepdims=True)
    summed = jnp.sum(jnp.exp(masked - top), axis=0, keepdims=True)
    positive = jnp.sum(jnp.where(hit, total, 0.0), axis=0, keepdims=True)
    rest = jnp.zeros((5,) + top.shape[1:], F32)
    packed = jnp.concatenate([top, summed, positive, rest], axis=0)
    stats[...] = jnp.broadcast_to(packed[None], stats.shape)


def grad_kernel(
    sizes, place, stats, score, full, passages, query_cells, positives, loss, send, keep, grads
):
    width = sizes[0]
    top, summed, positive = stats[:, 0, :], stats[:, 1, :], stats[:, 2, :]
    upper = jnp.max(top, axis=0, keepdims=True)
    total = jnp.sum(summed * jnp.exp(top - upper), axis=0, keepdims=True)
    lse = upper + jnp.log(total)
    loss[...] = lse - jnp.sum(positive, axis=0, keepdims=True)
    hit, allowed = masks(place, passages, query_cells, positives, sizes)
    masked = jnp.where(allowed, score[...], FAR)
    prob = jnp.exp(masked - lse) - jnp.where(hit, 1.0, 0.0)
    turned_prob = prob.T.astype(BF16)
    prob = prob.astype(BF16)
    factor = width**-0.5
    sections, count, rows, wide = keep.shape
    core = place[3]
    for j in range(count):
        for ref, c in ((keep, core), (send, 1 - core)):
            at = pl.ds(pl.multiple_of((2 * j + c) * wide, wide), wide)
            part = jnp.dot(turned_prob, passages[:, at], preferred_element_type=F32) * factor
            part = part.astype(BF16)
            for s in range(sections):
                ref[s, j] = part[s * rows : (s + 1) * rows]
    for j in range(0, width, wide):
        part = jnp.dot(prob, full[:, j : j + wide], preferred_element_type=F32) * factor
        part = part.astype(BF16)
        cycle, block = grads.shape[:2]
        for d in range(cycle):
            grads[d, :, j : j + wide] = part[d * block : (d + 1) * block]


def call(kernel, outs, args, loose=(), scratch=(), far_off=()):
    specs = [SMEM] + [VMEM] * (len(args) - 1) + [LOOSE] * len(loose)
    for k in far_off:
        specs[k] = LOOSE
    return pl.pallas_call(
        kernel,
        out_shape=[jax.ShapeDtypeStruct(shape, dtype) for shape, dtype in outs],
        in_specs=specs,
        out_specs=[VMEM] * len(outs),
        scratch_shapes=scratch,
        compiler_params=PARAMS,
        cost_estimate=COST,
    )(*args, *loose)


def shards(
    query_inputs,
    section_weights,
    head_weight,
    passages,
    query_cells,
    passage_cells,
    positives,
    master,
    moment_one,
    moment_two,
):
    sections = lax.axis_size("section")
    cycle = lax.axis_size("dp")
    count = lax.axis_size("y")
    section_at = lax.axis_index("section")
    place = jnp.stack(
        [section_at, lax.axis_index("dp"), lax.axis_index("y"), lax.axis_index("core")]
    ).astype(jnp.int32)
    queries, wide = query_inputs.shape
    block, width = passages.shape
    sizes = (width, cycle, 2 * count, block)
    rows = queries // sections
    taken = width // cycle
    with jax.named_scope("passages"):
        cells = jnp.broadcast_to(passage_cells.astype(BF16)[:, None], (block, queries))
        own = jnp.concatenate([passages, cells], axis=1)
        held = lax.all_gather(own, "dp", axis=0, tiled=True)
    section_weights = pltpu.with_memory_space_constraint(section_weights, pltpu.HBM)
    head_weight = pltpu.with_memory_space_constraint(head_weight, pltpu.HBM)
    local = query_inputs
    for layer in range(sections):
        with jax.named_scope("tower"):
            after = [local, held] if layer + 2 == sections else [local]
            layer_weight = loaded(place, section_weights, after)
            near, far = spread_after(local, place, [layer_weight])
            (local,) = call(
                layer_kernel,
                [((queries, wide), BF16)],
                [place, near, far, layer_weight],
            )
            if layer + 1 < sections:
                local = turned(local, "section", 1)
    with jax.named_scope("to_sections"):
        last = sections - 1
        final = jnp.where(section_at == last, local, 0).astype(BF16)
        for other in range(last):
            final = final + lax.ppermute(local, "section", [(last, other)])
    with jax.named_scope("head"):
        head_weight = loaded(place, head_weight, [final])
        near, far = spread_after(final, place, [head_weight])
        query_cols, slope, pieces = call(
            head_kernel,
            [
                ((queries, wide), BF16),
                ((queries, wide), F32),
                ((cycle, rows, taken), BF16),
            ],
            [place, near, far, head_weight],
            scratch=[pltpu.VMEM((queries, width), BF16)],
        )
    with jax.named_scope("normed_home"):
        pieces = lax.all_to_all(pieces, "dp", 0, 0)
    with jax.named_scope("score"):
        near, far = spread_after(query_cols, place, [pieces])
        row_cells, row_positives = query_cells[None, :], positives[None, :]
        group = sections * count * 2
        score, stats, full = call(
            functools.partial(score_kernel, sizes),
            [
                ((cycle * block, queries), F32),
                ((group, 8, queries), F32),
                ((queries, width), BF16),
            ],
            [place, near, far, held, row_cells, row_positives],
        )
    with jax.named_scope("stats"):
        stats = lax.all_to_all(stats, ("section", "y", "core"), 0, 0)
    with jax.named_scope("grad"):
        part = (sections, count, rows, wide)
        loss, send, keep, grads = call(
            functools.partial(grad_kernel, sizes),
            [((1, queries), F32), (part, BF16), (part, BF16), ((cycle, block, width), BF16)],
            [place, stats, score, full, held, row_cells, row_positives],
        )
    with jax.named_scope("passage_grads"):
        passage_grads = lax.psum_scatter(
            grads.reshape(cycle * block, width), "dp", scatter_dimension=0, tiled=True
        )
    with jax.named_scope("query_grad"):
        keep = (keep.astype(F32) + turned(send, "core", 1).astype(F32)).astype(BF16)
        parts = lax.all_to_all(keep.reshape(sections * count, rows, wide), ("section", "y"), 0, 0)
        (head_grad,) = call(
            head_grad_kernel, [((cycle, rows, wide), BF16)], [place, parts, slope]
        )
        head_grad = lax.all_to_all(head_grad, "dp", 0, 0)
    with jax.named_scope("weight_grad"):
        (part,) = call(
            weight_grad_kernel,
            [((sections, taken // sections, wide), BF16)],
            [place, head_grad, pieces],
        )
        part = lax.all_to_all(part, "section", 0, 0)
        tile = (master.shape, F32)
        new_master, new_moment_one, new_moment_two, passage_grads = call(
            update_kernel,
            [tile, tile, tile, ((block, width), F32)],
            [place, part, master, moment_one, moment_two, passage_grads],
        )
    return (loss[0], passage_grads, new_master, new_moment_one, new_moment_two)


def solution(mesh):
    sections, cycle, parts = (mesh.shape[axis] for axis in ("section", "dp", "mp"))
    split = Mesh(
        mesh.devices.reshape(sections, cycle, parts // 2, 2), ("section", "dp", "y", "core")
    )
    mp = ("y", "core")
    everything = ("section", "dp") + mp
    tile = P(("section", "dp"), mp)
    return jax.shard_map(
        shards,
        mesh=split,
        in_specs=(
            P("dp", mp),
            P("section", mp),
            P(None, mp),
            P(everything, None),
            P("dp"),
            P(everything),
            P("dp"),
            tile,
            tile,
            tile,
        ),
        out_specs=(P("dp"), P(everything, None), tile, tile, tile),
        check_vma=False,
    )
```

```python
import functools

import jax
import jax.numpy as jnp
from jax import lax
from jax.experimental import pallas as pl
from jax.experimental.pallas import tpu as pltpu
from jax.sharding import Mesh, PartitionSpec as P

correct_one = 0.9999734386011124
correct_two = 0.994079470779666
FAR = -1e30
F32 = jnp.float32
BF16 = jnp.bfloat16
VMEM = pl.BlockSpec(memory_space=pltpu.VMEM)
SMEM = pl.BlockSpec(memory_space=pltpu.SMEM)
LOOSE = pl.BlockSpec(memory_space=pltpu.HBM)
COST = pl.CostEstimate(flops=1024, bytes_accessed=1024, transcendentals=0)
PARAMS = pltpu.CompilerParams(vmem_limit_bytes=16 * 1024 * 1024)


def turned(block, axis, steps):
    count = lax.axis_size(axis)
    return lax.ppermute(block, axis, [(i, (i + steps) % count) for i in range(count)])


def spread(block):
    count = lax.axis_size("y")
    near = jnp.stack([block] + [turned(block, "y", k) for k in range(1, count)])
    return near, turned(near, "core", 1)


def stack_kernel(place, *rest):
    out = rest[-1]
    for k in range(out.shape[0]):
        out[k] = rest[k][...]


def spread_after(block, place, loose):
    if not loose:
        return spread(block)
    count = lax.axis_size("y")
    blocks = [block] + [turned(block, "y", k) for k in range(1, count)]
    (near,) = call(stack_kernel, [((count,) + block.shape, block.dtype)], [place] + blocks, loose)
    return near, turned(near, "core", 1)


def silu(u):
    return u * jax.nn.sigmoid(u)


def owners(place, ref, same):
    count = ref.shape[0]
    core = place[3] if same else 1 - place[3]
    return [lax.rem(place[2] - k + count, count) * 2 + core for k in range(count)]


def at_block(owner, wide):
    return pl.ds(pl.multiple_of(owner * wide, wide), wide)


def mixed_part(place, ref, same, weight):
    total = square = 0.0
    for k, owner in enumerate(owners(place, ref, same)):
        wide = ref[k].astype(F32)
        square = square + jnp.sum(wide * wide, axis=1, keepdims=True)
        rows = weight[at_block(owner, ref.shape[2]), :]
        total = total + jnp.dot(ref[k], rows, preferred_element_type=F32)
    return total, square


def near_kernel(place, near, weight, part, squares):
    total, square = mixed_part(place, near, True, weight)
    part[...] = total
    squares[...] = jnp.broadcast_to(square, squares.shape)


def mixed_rows(place, near, far, weight, part, squares):
    total, square = mixed_part(place, far, False, weight)
    width = 2 * near.shape[0] * near.shape[2]
    scale = lax.rsqrt((square + squares[:, :1]) / width + 1e-06)
    return (part[...] + total) * scale, scale


def load_kernel(place, source, *rest):
    out, sem = rest[-2:]
    copy = pltpu.make_async_copy(source, out, sem)
    copy.start()
    copy.wait()


def loaded(place, weight, after):
    (out,) = call(
        load_kernel,
        [(weight.shape, weight.dtype)],
        [place, weight],
        after,
        scratch=[pltpu.SemaphoreType.DMA],
        far_off=(1,),
    )
    return out


def started(place, near, weight):
    rows, wide = near.shape[1:]
    return call(near_kernel, [((rows, wide), F32), ((rows, 128), F32)], [place, near, weight])


def layer_kernel(place, near, far, weight, part, squares, out):
    mixed, _ = mixed_rows(place, near, far, weight, part, squares)
    out[...] = (near[0].astype(F32) + silu(mixed)).astype(BF16)


def head_kernel(place, near, far, weight, part, squares, emb, slope, pieces, normed):
    head, scale = mixed_rows(place, near, far, weight, part, squares)
    for ref, same in ((near, True), (far, False)):
        for k, owner in enumerate(owners(place, ref, same)):
            rows = (ref[k].astype(F32) * scale).astype(BF16)
            normed[:, at_block(owner, ref.shape[2])] = rows
    sig = jax.nn.sigmoid(head)
    emb[...] = (near[0].astype(F32) + head * sig).astype(BF16)
    slope[...] = sig * (1.0 + head * (1.0 - sig))
    cycle, rows, taken = pieces.shape
    taken -= 128
    shape = (rows, 128)
    row = lax.broadcasted_iota(jnp.int32, shape, 0)
    cells = jnp.zeros(shape, jnp.int32)
    for i in range(place.shape[0] - 4):
        cells = jnp.where(row == i, place[4 + i], cells)
    cells = cells.astype(F32).astype(BF16)
    sections = normed.shape[0] // rows
    piece = taken // sections
    own = pl.ds(pl.multiple_of(place[0] * rows, rows), rows)
    for k in range(cycle):
        pieces[k, :, taken:] = cells
        for s in range(sections):
            at = (s * cycle + k) * piece
            pieces[k, :, s * piece : (s + 1) * piece] = normed[own, at : at + piece]


def head_grad_kernel(place, parts, slope, out):
    cycle, rows, wide = out.shape
    total = 0.0
    for k in range(parts.shape[0]):
        total = total + parts[k].astype(F32)
    own = pl.ds(pl.multiple_of(place[0] * rows, rows), rows)
    grad = (total * slope[own, :]).astype(BF16)
    for k in range(cycle):
        out[k] = grad


def weight_grad_kernel(place, grads, pieces, out):
    cycle, rows, wide = grads.shape
    taken = out.shape[1]
    part = lax.dot_general(
        pieces[:, :, : pieces.shape[2] - 128].reshape(cycle * rows, pieces.shape[2] - 128),
        grads[...].reshape(cycle * rows, wide),
        (((0,), (0,)), ((), ())),
        preferred_element_type=F32,
    ).astype(BF16)
    for s in range(out.shape[0]):
        out[s] = part[s * taken : (s + 1) * taken]


def update_kernel(
    place, parts, master, moment_one, moment_two, grads, new_master, new_one, new_two, new_grads
):
    grad = 0.0
    for k in range(parts.shape[0]):
        grad = grad + parts[k].astype(F32)
    one = 0.9 * moment_one[...] + 0.1 * grad
    two = 0.95 * moment_two[...] + 0.05 * grad * grad
    update = one / correct_one / (jnp.sqrt(two / correct_two) + 1e-08)
    new_master[...] = master[...] - 0.001 * (update + 0.1 * master[...])
    new_one[...] = one
    new_two[...] = two
    new_grads[...] = grads[...].astype(F32)


def masks(place, pieces, query_cells, positives, sizes):
    width, cycle, parts, block = sizes
    rows, queries = cycle * block, positives.shape[1]
    at = lax.broadcasted_iota(jnp.int32, (rows, queries), 0)
    owner, inner = at // block, at % block
    part = place[2] * 2 + place[3]
    index = ((place[0] * cycle + owner) * parts + part) * block + inner
    hit = index == positives[...]
    first = pieces.shape[2] - 128
    cells = pieces[:, :block, first : first + queries].astype(F32).reshape(rows, queries)
    allowed = jnp.logical_or(hit, cells == query_cells[...].astype(F32))
    return hit, allowed


def score_kernel(
    sizes, place, near, far, passages, pieces, query_cells, positives, score, stats, full
):
    wide = near.shape[2]
    total = 0.0
    for ref, same in ((near, True), (far, False)):
        for k, owner in enumerate(owners(place, ref, same)):
            at = at_block(owner, wide)
            full[:, at] = ref[k]
            total = total + lax.dot_general(
                passages[:, at], ref[k], (((1,), (1,)), ((), ())), preferred_element_type=F32
            )
    total = total * sizes[0] ** -0.5
    score[...] = total
    hit, allowed = masks(place, pieces, query_cells, positives, sizes)
    masked = jnp.where(allowed, total, FAR)
    top = jnp.max(masked, axis=0, keepdims=True)
    summed = jnp.sum(jnp.exp(masked - top), axis=0, keepdims=True)
    positive = jnp.sum(jnp.where(hit, total, 0.0), axis=0, keepdims=True)
    rest = jnp.zeros((5,) + top.shape[1:], F32)
    packed = jnp.concatenate([top, summed, positive, rest], axis=0)
    stats[...] = jnp.broadcast_to(packed[None], stats.shape)


def grad_kernel(
    sizes, place, stats, score, full, passages, pieces, query_cells, positives,
    loss, send, keep, grads,
):
    width = sizes[0]
    top, summed, positive = stats[:, 0, :], stats[:, 1, :], stats[:, 2, :]
    upper = jnp.max(top, axis=0, keepdims=True)
    total = jnp.sum(summed * jnp.exp(top - upper), axis=0, keepdims=True)
    lse = upper + jnp.log(total)
    loss[...] = lse - jnp.sum(positive, axis=0, keepdims=True)
    hit, allowed = masks(place, pieces, query_cells, positives, sizes)
    masked = jnp.where(allowed, score[...], FAR)
    prob = jnp.exp(masked - lse) - jnp.where(hit, 1.0, 0.0)
    turned_prob = prob.T.astype(BF16)
    prob = prob.astype(BF16)
    factor = width**-0.5
    sections, count, rows, wide = keep.shape
    core = place[3]
    for j in range(count):
        for ref, c in ((keep, core), (send, 1 - core)):
            at = pl.ds(pl.multiple_of((2 * j + c) * wide, wide), wide)
            part = jnp.dot(turned_prob, passages[:, at], preferred_element_type=F32) * factor
            part = part.astype(BF16)
            for s in range(sections):
                ref[s, j] = part[s * rows : (s + 1) * rows]
    for j in range(0, width, wide):
        part = jnp.dot(prob, full[:, j : j + wide], preferred_element_type=F32) * factor
        part = part.astype(BF16)
        cycle, block = grads.shape[:2]
        for d in range(cycle):
            grads[d, :, j : j + wide] = part[d * block : (d + 1) * block]


def call(kernel, outs, args, loose=(), scratch=(), far_off=()):
    specs = [SMEM] + [VMEM] * (len(args) - 1) + [LOOSE] * len(loose)
    for k in far_off:
        specs[k] = LOOSE
    return pl.pallas_call(
        kernel,
        out_shape=[jax.ShapeDtypeStruct(shape, dtype) for shape, dtype in outs],
        in_specs=specs,
        out_specs=[VMEM] * len(outs),
        scratch_shapes=scratch,
        compiler_params=PARAMS,
        cost_estimate=COST,
    )(*args, *loose)


def shards(
    query_inputs,
    section_weights,
    head_weight,
    passages,
    query_cells,
    passage_cells,
    positives,
    master,
    moment_one,
    moment_two,
):
    sections = lax.axis_size("section")
    cycle = lax.axis_size("dp")
    count = lax.axis_size("y")
    section_at = lax.axis_index("section")
    place = [section_at, lax.axis_index("dp"), lax.axis_index("y"), lax.axis_index("core")]
    place = jnp.concatenate([jnp.stack(place).astype(jnp.int32), passage_cells])
    queries, wide = query_inputs.shape
    block, width = passages.shape
    sizes = (width, cycle, 2 * count, block)
    rows = queries // sections
    taken = width // cycle
    with jax.named_scope("passages"):
        held = lax.all_gather(passages, "dp", axis=0, tiled=True)
    section_weights = pltpu.with_memory_space_constraint(section_weights, pltpu.HBM)
    head_weight = pltpu.with_memory_space_constraint(head_weight, pltpu.HBM)
    arrived = pltpu.with_memory_space_constraint(held, pltpu.HBM)
    local = query_inputs
    for layer in range(sections):
        with jax.named_scope("tower"):
            after = [local, arrived] if layer + 2 == sections else [local]
            layer_weight = loaded(place, section_weights, after)
            near, far = spread_after(local, place, [layer_weight])
            (local,) = call(
                layer_kernel,
                [((queries, wide), BF16)],
                [place, near, far, layer_weight, *started(place, near, layer_weight)],
            )
            if layer + 1 < sections:
                local = turned(local, "section", 1)
    with jax.named_scope("to_sections"):
        last = sections - 1
        final = jnp.where(section_at == last, local, 0).astype(BF16)
        for other in range(last):
            final = final + lax.ppermute(local, "section", [(last, other)])
    with jax.named_scope("head"):
        head_weight = loaded(place, head_weight, [final])
        near, far = spread_after(final, place, [head_weight])
        query_cols, slope, pieces = call(
            head_kernel,
            [
                ((queries, wide), BF16),
                ((queries, wide), F32),
                ((cycle, rows, taken + 128), BF16),
            ],
            [place, near, far, head_weight, *started(place, near, head_weight)],
            scratch=[pltpu.VMEM((queries, width), BF16)],
        )
    with jax.named_scope("normed_home"):
        pieces = lax.all_to_all(pieces, "dp", 0, 0)
    with jax.named_scope("score"):
        near, far = spread_after(query_cols, place, [pieces])
        row_cells, row_positives = query_cells[None, :], positives[None, :]
        group = sections * count * 2
        score, stats, full = call(
            functools.partial(score_kernel, sizes),
            [
                ((cycle * block, queries), F32),
                ((group, 8, queries), F32),
                ((queries, width), BF16),
            ],
            [place, near, far, held, pieces, row_cells, row_positives],
        )
    with jax.named_scope("stats"):
        stats = lax.all_to_all(stats, ("section", "y", "core"), 0, 0)
    with jax.named_scope("grad"):
        part = (sections, count, rows, wide)
        loss, send, keep, grads = call(
            functools.partial(grad_kernel, sizes),
            [((1, queries), F32), (part, BF16), (part, BF16), ((cycle, block, width), BF16)],
            [place, stats, score, full, held, pieces, row_cells, row_positives],
        )
    with jax.named_scope("passage_grads"):
        passage_grads = lax.psum_scatter(
            grads.reshape(cycle * block, width), "dp", scatter_dimension=0, tiled=True
        )
    with jax.named_scope("query_grad"):
        keep = (keep.astype(F32) + turned(send, "core", 1).astype(F32)).astype(BF16)
        parts = lax.all_to_all(keep.reshape(sections * count, rows, wide), ("section", "y"), 0, 0)
        (head_grad,) = call(
            head_grad_kernel, [((cycle, rows, wide), BF16)], [place, parts, slope]
        )
        head_grad = lax.all_to_all(head_grad, "dp", 0, 0)
    with jax.named_scope("weight_grad"):
        (part,) = call(
            weight_grad_kernel,
            [((sections, taken // sections, wide), BF16)],
            [place, head_grad, pieces],
        )
        part = lax.all_to_all(part, "section", 0, 0)
        tile = (master.shape, F32)
        new_master, new_moment_one, new_moment_two, passage_grads = call(
            update_kernel,
            [tile, tile, tile, ((block, width), F32)],
            [place, part, master, moment_one, moment_two, passage_grads],
        )
    return (loss[0], passage_grads, new_master, new_moment_one, new_moment_two)


def solution(mesh):
    sections, cycle, parts = (mesh.shape[axis] for axis in ("section", "dp", "mp"))
    split = Mesh(
        mesh.devices.reshape(sections, cycle, parts // 2, 2), ("section", "dp", "y", "core")
    )
    mp = ("y", "core")
    everything = ("section", "dp") + mp
    tile = P(("section", "dp"), mp)
    return jax.shard_map(
        shards,
        mesh=split,
        in_specs=(
            P("dp", mp),
            P("section", mp),
            P(None, mp),
            P(everything, None),
            P("dp"),
            P(everything),
            P("dp"),
            tile,
            tile,
            tile,
        ),
        out_specs=(P("dp"), P(everything, None), tile, tile, tile),
        check_vma=False,
    )
```

```python
import functools

import jax
import jax.numpy as jnp
from jax import lax
from jax.experimental import pallas as pl
from jax.experimental.pallas import tpu as pltpu
from jax.sharding import Mesh, PartitionSpec as P

correct_one = 0.9999734386011124
correct_two = 0.994079470779666
FAR = -1e30
F32 = jnp.float32
BF16 = jnp.bfloat16
VMEM = pl.BlockSpec(memory_space=pltpu.VMEM)
SMEM = pl.BlockSpec(memory_space=pltpu.SMEM)
LOOSE = pl.BlockSpec(memory_space=pltpu.HBM)
COST = pl.CostEstimate(flops=1024, bytes_accessed=1024, transcendentals=0)
PARAMS = pltpu.CompilerParams(vmem_limit_bytes=16 * 1024 * 1024)


def turned(block, axis, steps):
    count = lax.axis_size(axis)
    return lax.ppermute(block, axis, [(i, (i + steps) % count) for i in range(count)])


def spread(block):
    count = lax.axis_size("y")
    near = jnp.stack([block] + [turned(block, "y", k) for k in range(1, count)])
    return near, turned(near, "core", 1)


def spread_after(block, loose):
    if not loose:
        return spread(block)
    count = lax.axis_size("y")
    blocks = [block] + [turned(block, "y", k) for k in range(1, count)]
    blocks, _ = lax.optimization_barrier((blocks, loose))
    near = jnp.stack(blocks)
    return near, turned(near, "core", 1)


def silu(u):
    return u * jax.nn.sigmoid(u)


def owners(place, ref, same):
    count = ref.shape[0]
    core = place[3] if same else 1 - place[3]
    return [lax.rem(place[2] - k + count, count) * 2 + core for k in range(count)]


def at_block(owner, wide):
    return pl.ds(pl.multiple_of(owner * wide, wide), wide)


def mixed_part(place, ref, same, weight):
    total = square = 0.0
    for k, owner in enumerate(owners(place, ref, same)):
        wide = ref[k].astype(F32)
        square = square + jnp.sum(wide * wide, axis=1, keepdims=True)
        rows = weight[at_block(owner, ref.shape[2]), :]
        total = total + jnp.dot(ref[k], rows, preferred_element_type=F32)
    return total, square


def near_kernel(place, near, weight, part, squares):
    total, square = mixed_part(place, near, True, weight)
    part[...] = total
    squares[...] = jnp.broadcast_to(square, squares.shape)


def mixed_rows(place, near, far, weight, part, squares):
    total, square = mixed_part(place, far, False, weight)
    width = 2 * near.shape[0] * near.shape[2]
    scale = lax.rsqrt((square + squares[:, :1]) / width + 1e-06)
    return (part[...] + total) * scale, scale


def load_kernel(place, source, *rest):
    out, sem = rest[-2:]
    copy = pltpu.make_async_copy(source, out, sem)
    copy.start()
    copy.wait()


def loaded(place, weight, after):
    (out,) = call(
        load_kernel,
        [(weight.shape, weight.dtype)],
        [place, weight],
        after,
        scratch=[pltpu.SemaphoreType.DMA],
        far_off=(1,),
    )
    return out


def started(place, near, weight):
    rows, wide = near.shape[1:]
    return call(near_kernel, [((rows, wide), F32), ((rows, 128), F32)], [place, near, weight])


def layer_kernel(place, near, far, weight, part, squares, out):
    mixed, _ = mixed_rows(place, near, far, weight, part, squares)
    out[...] = (near[0].astype(F32) + silu(mixed)).astype(BF16)


def head_kernel(place, near, far, weight, part, squares, emb, slope, pieces, normed):
    head, scale = mixed_rows(place, near, far, weight, part, squares)
    for ref, same in ((near, True), (far, False)):
        for k, owner in enumerate(owners(place, ref, same)):
            rows = (ref[k].astype(F32) * scale).astype(BF16)
            normed[:, at_block(owner, ref.shape[2])] = rows
    sig = jax.nn.sigmoid(head)
    emb[...] = (near[0].astype(F32) + head * sig).astype(BF16)
    slope[...] = sig * (1.0 + head * (1.0 - sig))
    cycle, rows, taken = pieces.shape
    taken -= 128
    shape = (rows, 128)
    row = lax.broadcasted_iota(jnp.int32, shape, 0)
    cells = jnp.zeros(shape, jnp.int32)
    for i in range(place.shape[0] - 4):
        cells = jnp.where(row == i, place[4 + i], cells)
    cells = cells.astype(F32).astype(BF16)
    sections = normed.shape[0] // rows
    piece = taken // sections
    own = pl.ds(pl.multiple_of(place[0] * rows, rows), rows)
    for k in range(cycle):
        pieces[k, :, taken:] = cells
        for s in range(sections):
            at = (s * cycle + k) * piece
            pieces[k, :, s * piece : (s + 1) * piece] = normed[own, at : at + piece]


def head_grad_kernel(place, parts, slope, out):
    cycle, rows, wide = out.shape
    total = 0.0
    for k in range(parts.shape[0]):
        total = total + parts[k].astype(F32)
    own = pl.ds(pl.multiple_of(place[0] * rows, rows), rows)
    grad = (total * slope[own, :]).astype(BF16)
    for k in range(cycle):
        out[k] = grad


def weight_grad_kernel(place, grads, pieces, out):
    cycle, rows, wide = grads.shape
    taken = out.shape[1]
    part = lax.dot_general(
        pieces[:, :, : pieces.shape[2] - 128].reshape(cycle * rows, pieces.shape[2] - 128),
        grads[...].reshape(cycle * rows, wide),
        (((0,), (0,)), ((), ())),
        preferred_element_type=F32,
    ).astype(BF16)
    for s in range(out.shape[0]):
        out[s] = part[s * taken : (s + 1) * taken]


def update_kernel(
    place, parts, master, moment_one, moment_two, grads,
    new_master, new_one, new_two, new_grads, held, sem,
):
    copy = pltpu.make_async_copy(grads, held, sem)
    copy.start()
    grad = 0.0
    for k in range(parts.shape[0]):
        grad = grad + parts[k].astype(F32)
    one = 0.9 * moment_one[...] + 0.1 * grad
    two = 0.95 * moment_two[...] + 0.05 * grad * grad
    update = one / correct_one / (jnp.sqrt(two / correct_two) + 1e-08)
    new_master[...] = master[...] - 0.001 * (update + 0.1 * master[...])
    new_one[...] = one
    new_two[...] = two
    copy.wait()
    new_grads[...] = held[...].astype(F32)


def masks(place, pieces, query_cells, positives, sizes):
    width, cycle, parts, block = sizes
    rows, queries = cycle * block, positives.shape[1]
    at = lax.broadcasted_iota(jnp.int32, (rows, queries), 0)
    owner, inner = at // block, at % block
    part = place[2] * 2 + place[3]
    index = ((place[0] * cycle + owner) * parts + part) * block + inner
    hit = index == positives[...]
    first = pieces.shape[2] - 128
    cells = pieces[:, :block, first : first + queries].astype(F32).reshape(rows, queries)
    allowed = jnp.logical_or(hit, cells == query_cells[...].astype(F32))
    return hit, allowed


def score_kernel(
    sizes, place, near, far, passages, pieces, query_cells, positives, score, stats, full
):
    wide = near.shape[2]
    total = 0.0
    for ref, same in ((near, True), (far, False)):
        for k, owner in enumerate(owners(place, ref, same)):
            at = at_block(owner, wide)
            full[:, at] = ref[k]
            total = total + lax.dot_general(
                passages[:, at], ref[k], (((1,), (1,)), ((), ())), preferred_element_type=F32
            )
    total = total * sizes[0] ** -0.5
    score[...] = total
    hit, allowed = masks(place, pieces, query_cells, positives, sizes)
    masked = jnp.where(allowed, total, FAR)
    top = jnp.max(masked, axis=0, keepdims=True)
    summed = jnp.sum(jnp.exp(masked - top), axis=0, keepdims=True)
    positive = jnp.sum(jnp.where(hit, total, 0.0), axis=0, keepdims=True)
    rest = jnp.zeros((5,) + top.shape[1:], F32)
    packed = jnp.concatenate([top, summed, positive, rest], axis=0)
    stats[...] = jnp.broadcast_to(packed[None], stats.shape)


def grad_kernel(
    sizes, place, stats, score, full, passages, pieces, query_cells, positives,
    loss, send, keep, grads,
):
    width = sizes[0]
    top, summed, positive = stats[:, 0, :], stats[:, 1, :], stats[:, 2, :]
    upper = jnp.max(top, axis=0, keepdims=True)
    total = jnp.sum(summed * jnp.exp(top - upper), axis=0, keepdims=True)
    lse = upper + jnp.log(total)
    loss[...] = lse - jnp.sum(positive, axis=0, keepdims=True)
    hit, allowed = masks(place, pieces, query_cells, positives, sizes)
    masked = jnp.where(allowed, score[...], FAR)
    prob = jnp.exp(masked - lse) - jnp.where(hit, 1.0, 0.0)
    turned_prob = prob.T.astype(BF16)
    prob = prob.astype(BF16)
    factor = width**-0.5
    sections, count, rows, wide = keep.shape
    core = place[3]
    for j in range(count):
        for ref, c in ((keep, core), (send, 1 - core)):
            at = pl.ds(pl.multiple_of((2 * j + c) * wide, wide), wide)
            part = jnp.dot(turned_prob, passages[:, at], preferred_element_type=F32) * factor
            part = part.astype(BF16)
            for s in range(sections):
                ref[s, j] = part[s * rows : (s + 1) * rows]
    for j in range(0, width, wide):
        part = jnp.dot(prob, full[:, j : j + wide], preferred_element_type=F32) * factor
        part = part.astype(BF16)
        cycle, block = grads.shape[:2]
        for d in range(cycle):
            grads[d, :, j : j + wide] = part[d * block : (d + 1) * block]


def call(kernel, outs, args, loose=(), scratch=(), far_off=()):
    specs = [SMEM] + [VMEM] * (len(args) - 1) + [LOOSE] * len(loose)
    for k in far_off:
        specs[k] = LOOSE
    return pl.pallas_call(
        kernel,
        out_shape=[jax.ShapeDtypeStruct(shape, dtype) for shape, dtype in outs],
        in_specs=specs,
        out_specs=[VMEM] * len(outs),
        scratch_shapes=scratch,
        compiler_params=PARAMS,
        cost_estimate=COST,
    )(*args, *loose)


def shards(
    query_inputs,
    section_weights,
    head_weight,
    passages,
    query_cells,
    passage_cells,
    positives,
    master,
    moment_one,
    moment_two,
):
    sections = lax.axis_size("section")
    cycle = lax.axis_size("dp")
    count = lax.axis_size("y")
    section_at = lax.axis_index("section")
    place = [section_at, lax.axis_index("dp"), lax.axis_index("y"), lax.axis_index("core")]
    place = jnp.concatenate([jnp.stack(place).astype(jnp.int32), passage_cells])
    queries, wide = query_inputs.shape
    block, width = passages.shape
    sizes = (width, cycle, 2 * count, block)
    rows = queries // sections
    taken = width // cycle
    with jax.named_scope("passages"):
        held = lax.all_gather(passages, "dp", axis=0, tiled=True)
    section_weights = pltpu.with_memory_space_constraint(section_weights, pltpu.HBM)
    head_weight = pltpu.with_memory_space_constraint(head_weight, pltpu.HBM)
    arrived = pltpu.with_memory_space_constraint(held, pltpu.HBM)
    local = query_inputs
    for layer in range(sections):
        with jax.named_scope("tower"):
            after = [local, arrived] if layer + 2 == sections else [local]
            layer_weight = loaded(place, section_weights, after)
            near, far = spread_after(local, [layer_weight])
            (local,) = call(
                layer_kernel,
                [((queries, wide), BF16)],
                [place, near, far, layer_weight, *started(place, near, layer_weight)],
            )
            if layer + 1 < sections:
                local = turned(local, "section", 1)
    with jax.named_scope("to_sections"):
        last = sections - 1
        final = jnp.where(section_at == last, local, 0).astype(BF16)
        for other in range(last):
            final = final + lax.ppermute(local, "section", [(last, other)])
    with jax.named_scope("head"):
        head_weight = loaded(place, head_weight, [final])
        near, far = spread_after(final, [head_weight])
        query_cols, slope, pieces = call(
            head_kernel,
            [
                ((queries, wide), BF16),
                ((queries, wide), F32),
                ((cycle, rows, taken + 128), BF16),
            ],
            [place, near, far, head_weight, *started(place, near, head_weight)],
            scratch=[pltpu.VMEM((queries, width), BF16)],
        )
    with jax.named_scope("normed_home"):
        pieces = lax.all_to_all(pieces, "dp", 0, 0)
    with jax.named_scope("score"):
        near, far = spread_after(query_cols, [pieces])
        row_cells, row_positives = query_cells[None, :], positives[None, :]
        group = sections * count * 2
        score, stats, full = call(
            functools.partial(score_kernel, sizes),
            [
                ((cycle * block, queries), F32),
                ((group, 8, queries), F32),
                ((queries, width), BF16),
            ],
            [place, near, far, held, pieces, row_cells, row_positives],
        )
    with jax.named_scope("stats"):
        stats = lax.all_to_all(stats, ("section", "y", "core"), 0, 0)
    with jax.named_scope("grad"):
        part = (sections, count, rows, wide)
        loss, send, keep, grads = call(
            functools.partial(grad_kernel, sizes),
            [((1, queries), F32), (part, BF16), (part, BF16), ((cycle, block, width), BF16)],
            [place, stats, score, full, held, pieces, row_cells, row_positives],
        )
    with jax.named_scope("passage_grads"):
        passage_grads = lax.psum_scatter(
            grads.reshape(cycle * block, width), "dp", scatter_dimension=0, tiled=True
        )
    with jax.named_scope("query_grad"):
        keep = (keep.astype(F32) + turned(send, "core", 1).astype(F32)).astype(BF16)
        parts = lax.all_to_all(keep.reshape(sections * count, rows, wide), ("section", "y"), 0, 0)
        (head_grad,) = call(
            head_grad_kernel, [((cycle, rows, wide), BF16)], [place, parts, slope]
        )
        head_grad = lax.all_to_all(head_grad, "dp", 0, 0)
    with jax.named_scope("weight_grad"):
        (part,) = call(
            weight_grad_kernel,
            [((sections, taken // sections, wide), BF16)],
            [place, head_grad, pieces],
        )
        part = lax.all_to_all(part, "section", 0, 0)
        tile = (master.shape, F32)
        new_master, new_moment_one, new_moment_two, passage_grads = call(
            update_kernel,
            [tile, tile, tile, ((block, width), F32)],
            [
                place, part, master, moment_one, moment_two,
                pltpu.with_memory_space_constraint(passage_grads, pltpu.HBM),
            ],
            scratch=[pltpu.VMEM((block, width), BF16), pltpu.SemaphoreType.DMA],
            far_off=(5,),
        )
    return (loss[0], passage_grads, new_master, new_moment_one, new_moment_two)


def solution(mesh):
    sections, cycle, parts = (mesh.shape[axis] for axis in ("section", "dp", "mp"))
    split = Mesh(
        mesh.devices.reshape(sections, cycle, parts // 2, 2), ("section", "dp", "y", "core")
    )
    mp = ("y", "core")
    everything = ("section", "dp") + mp
    tile = P(("section", "dp"), mp)
    return jax.shard_map(
        shards,
        mesh=split,
        in_specs=(
            P("dp", mp),
            P("section", mp),
            P(None, mp),
            P(everything, None),
            P("dp"),
            P(everything),
            P("dp"),
            tile,
            tile,
            tile,
        ),
        out_specs=(P("dp"), P(everything, None), tile, tile, tile),
        check_vma=False,
    )
```

```python
import functools

import jax
import jax.numpy as jnp
from jax import lax
from jax.experimental import pallas as pl
from jax.experimental.pallas import tpu as pltpu
from jax.sharding import Mesh, PartitionSpec as P

correct_one = 0.9999734386011124
correct_two = 0.994079470779666
FAR = -1e30
F32 = jnp.float32
BF16 = jnp.bfloat16
VMEM = pl.BlockSpec(memory_space=pltpu.VMEM)
SMEM = pl.BlockSpec(memory_space=pltpu.SMEM)
LOOSE = pl.BlockSpec(memory_space=pltpu.HBM)
COST = pl.CostEstimate(flops=1024, bytes_accessed=1024, transcendentals=0)
PARAMS = pltpu.CompilerParams(vmem_limit_bytes=16 * 1024 * 1024)


def turned(block, axis, steps):
    count = lax.axis_size(axis)
    return lax.ppermute(block, axis, [(i, (i + steps) % count) for i in range(count)])


def spread(block):
    count = lax.axis_size("y")
    near = jnp.stack([block] + [turned(block, "y", k) for k in range(1, count)])
    return near, turned(near, "core", 1)


def spread_after(block, loose):
    if not loose:
        return spread(block)
    count = lax.axis_size("y")
    blocks = [block] + [turned(block, "y", k) for k in range(1, count)]
    blocks, _ = lax.optimization_barrier((blocks, loose))
    near = jnp.stack(blocks)
    return near, turned(near, "core", 1)


def silu(u):
    return u * jax.nn.sigmoid(u)


def owners(place, ref, same):
    count = ref.shape[0]
    core = place[3] if same else 1 - place[3]
    return [lax.rem(place[2] - k + count, count) * 2 + core for k in range(count)]


def at_block(owner, wide):
    return pl.ds(pl.multiple_of(owner * wide, wide), wide)


def mixed_part(place, ref, same, weight):
    total = square = 0.0
    for k, owner in enumerate(owners(place, ref, same)):
        wide = ref[k].astype(F32)
        square = square + jnp.sum(wide * wide, axis=1, keepdims=True)
        rows = weight[at_block(owner, ref.shape[2]), :]
        total = total + jnp.dot(ref[k], rows, preferred_element_type=F32)
    return total, square


def near_kernel(place, near, weight, part, squares):
    total, square = mixed_part(place, near, True, weight)
    part[...] = total
    squares[...] = jnp.broadcast_to(square, squares.shape)


def mixed_rows(place, near, far, weight, part, squares):
    total, square = mixed_part(place, far, False, weight)
    width = 2 * near.shape[0] * near.shape[2]
    scale = lax.rsqrt((square + squares[:, :1]) / width + 1e-06)
    return (part[...] + total) * scale, scale


def load_kernel(place, source, *rest):
    out, sem = rest[-2:]
    copy = pltpu.make_async_copy(source, out, sem)
    copy.start()
    copy.wait()


def loaded(place, weight, after):
    (out,) = call(
        load_kernel,
        [(weight.shape, weight.dtype)],
        [place, weight],
        after,
        scratch=[pltpu.SemaphoreType.DMA],
        far_off=(1,),
    )
    return out


def started(place, near, weight):
    rows, wide = near.shape[1:]
    return call(near_kernel, [((rows, wide), F32), ((rows, 128), F32)], [place, near, weight])


def layer_kernel(place, near, far, weight, part, squares, out):
    mixed, _ = mixed_rows(place, near, far, weight, part, squares)
    out[...] = (near[0].astype(F32) + silu(mixed)).astype(BF16)


def head_kernel(place, near, far, weight, part, squares, emb, slope, pieces, normed):
    head, scale = mixed_rows(place, near, far, weight, part, squares)
    for ref, same in ((near, True), (far, False)):
        for k, owner in enumerate(owners(place, ref, same)):
            rows = (ref[k].astype(F32) * scale).astype(BF16)
            normed[:, at_block(owner, ref.shape[2])] = rows
    sig = jax.nn.sigmoid(head)
    emb[...] = (near[0].astype(F32) + head * sig).astype(BF16)
    slope[...] = sig * (1.0 + head * (1.0 - sig))
    cycle, rows, taken = pieces.shape
    taken -= 128
    shape = (rows, 128)
    row = lax.broadcasted_iota(jnp.int32, shape, 0)
    cells = jnp.zeros(shape, jnp.int32)
    for i in range(place.shape[0] - 4):
        cells = jnp.where(row == i, place[4 + i], cells)
    cells = cells.astype(F32).astype(BF16)
    sections = normed.shape[0] // rows
    piece = taken // sections
    own = pl.ds(pl.multiple_of(place[0] * rows, rows), rows)
    for k in range(cycle):
        pieces[k, :, taken:] = cells
        for s in range(sections):
            at = (s * cycle + k) * piece
            pieces[k, :, s * piece : (s + 1) * piece] = normed[own, at : at + piece]


def head_grad_kernel(place, parts, slope, out):
    cycle, rows, wide = out.shape
    total = 0.0
    for k in range(parts.shape[0]):
        total = total + parts[k].astype(F32)
    own = pl.ds(pl.multiple_of(place[0] * rows, rows), rows)
    grad = (total * slope[own, :]).astype(BF16)
    for k in range(cycle):
        out[k] = grad


def weight_grad_kernel(place, grads, pieces, out):
    cycle, rows, wide = grads.shape
    taken = out.shape[1]
    part = lax.dot_general(
        pieces[:, :, : pieces.shape[2] - 128].reshape(cycle * rows, pieces.shape[2] - 128),
        grads[...].reshape(cycle * rows, wide),
        (((0,), (0,)), ((), ())),
        preferred_element_type=F32,
    ).astype(BF16)
    for s in range(out.shape[0]):
        out[s] = part[s * taken : (s + 1) * taken]


def update_kernel(
    place, parts, master, moment_one, moment_two, grads,
    new_master, new_one, new_two, new_grads, held, sem,
):
    copy = pltpu.make_async_copy(grads, held, sem)
    copy.start()
    grad = 0.0
    for k in range(parts.shape[0]):
        grad = grad + parts[k].astype(F32)
    one = 0.9 * moment_one[...] + 0.1 * grad
    two = 0.95 * moment_two[...] + 0.05 * grad * grad
    update = one / correct_one / (jnp.sqrt(two / correct_two) + 1e-08)
    new_master[...] = master[...] - 0.001 * (update + 0.1 * master[...])
    new_one[...] = one
    new_two[...] = two
    copy.wait()
    new_grads[...] = held[...].astype(F32)


def masks(place, pieces, query_cells, positives, sizes):
    width, cycle, parts, block = sizes
    rows, queries = cycle * block, positives.shape[1]
    at = lax.broadcasted_iota(jnp.int32, (rows, queries), 0)
    owner, inner = at // block, at % block
    part = place[2] * 2 + place[3]
    index = ((place[0] * cycle + owner) * parts + part) * block + inner
    hit = index == positives[...]
    first = pieces.shape[2] - 128
    cells = pieces[:, :block, first : first + queries].astype(F32).reshape(rows, queries)
    allowed = jnp.logical_or(hit, cells == query_cells[...].astype(F32))
    return hit, allowed


def score_kernel(
    sizes, place, near, far, passages, pieces, query_cells, positives, score, stats, full
):
    wide = near.shape[2]
    total = 0.0
    for ref, same in ((near, True), (far, False)):
        for k, owner in enumerate(owners(place, ref, same)):
            at = at_block(owner, wide)
            full[:, at] = ref[k]
            total = total + lax.dot_general(
                passages[:, at], ref[k], (((1,), (1,)), ((), ())), preferred_element_type=F32
            )
    total = total * sizes[0] ** -0.5
    score[...] = total
    hit, allowed = masks(place, pieces, query_cells, positives, sizes)
    masked = jnp.where(allowed, total, FAR)
    top = jnp.max(masked, axis=0, keepdims=True)
    summed = jnp.sum(jnp.exp(masked - top), axis=0, keepdims=True)
    positive = jnp.sum(jnp.where(hit, total, 0.0), axis=0, keepdims=True)
    rest = jnp.zeros((5,) + top.shape[1:], F32)
    packed = jnp.concatenate([top, summed, positive, rest], axis=0)
    stats[...] = jnp.broadcast_to(packed[None], stats.shape)


def grad_kernel(
    sizes, place, stats, score, passages, pieces, query_cells, positives,
    loss, send, prob_out, turned_out,
):
    width = sizes[0]
    top, summed, positive = stats[:, 0, :], stats[:, 1, :], stats[:, 2, :]
    upper = jnp.max(top, axis=0, keepdims=True)
    total = jnp.sum(summed * jnp.exp(top - upper), axis=0, keepdims=True)
    lse = upper + jnp.log(total)
    loss[...] = lse - jnp.sum(positive, axis=0, keepdims=True)
    hit, allowed = masks(place, pieces, query_cells, positives, sizes)
    masked = jnp.where(allowed, score[...], FAR)
    prob = jnp.exp(masked - lse) - jnp.where(hit, 1.0, 0.0)
    turned_prob = prob.T.astype(BF16)
    prob_out[...] = prob.astype(BF16)
    turned_out[...] = turned_prob
    query_parts(turned_prob, passages, send, 1 - place[3], width)


def query_parts(turned_prob, passages, out, core, width):
    sections, count, rows, wide = out.shape
    for j in range(count):
        at = at_block(2 * j + core, wide)
        part = jnp.dot(turned_prob, passages[:, at], preferred_element_type=F32) * width**-0.5
        part = part.astype(BF16)
        for s in range(sections):
            out[s, j] = part[s * rows : (s + 1) * rows]


def rest_kernel(sizes, place, prob, turned_prob, full, passages, keep, grads):
    width, wide = sizes[0], keep.shape[3]
    query_parts(turned_prob[...], passages, keep, place[3], width)
    cycle, block = grads.shape[:2]
    for j in range(0, width, wide):
        part = jnp.dot(prob[...], full[:, j : j + wide], preferred_element_type=F32)
        part = (part * width**-0.5).astype(BF16)
        for d in range(cycle):
            grads[d, :, j : j + wide] = part[d * block : (d + 1) * block]


def call(kernel, outs, args, loose=(), scratch=(), far_off=()):
    specs = [SMEM] + [VMEM] * (len(args) - 1) + [LOOSE] * len(loose)
    for k in far_off:
        specs[k] = LOOSE
    return pl.pallas_call(
        kernel,
        out_shape=[jax.ShapeDtypeStruct(shape, dtype) for shape, dtype in outs],
        in_specs=specs,
        out_specs=[VMEM] * len(outs),
        scratch_shapes=scratch,
        compiler_params=PARAMS,
        cost_estimate=COST,
    )(*args, *loose)


def shards(
    query_inputs,
    section_weights,
    head_weight,
    passages,
    query_cells,
    passage_cells,
    positives,
    master,
    moment_one,
    moment_two,
):
    sections = lax.axis_size("section")
    cycle = lax.axis_size("dp")
    count = lax.axis_size("y")
    section_at = lax.axis_index("section")
    place = [section_at, lax.axis_index("dp"), lax.axis_index("y"), lax.axis_index("core")]
    place = jnp.concatenate([jnp.stack(place).astype(jnp.int32), passage_cells])
    queries, wide = query_inputs.shape
    block, width = passages.shape
    sizes = (width, cycle, 2 * count, block)
    rows = queries // sections
    taken = width // cycle
    with jax.named_scope("passages"):
        held = lax.all_gather(passages, "dp", axis=0, tiled=True)
    section_weights = pltpu.with_memory_space_constraint(section_weights, pltpu.HBM)
    head_weight = pltpu.with_memory_space_constraint(head_weight, pltpu.HBM)
    arrived = pltpu.with_memory_space_constraint(held, pltpu.HBM)
    local = query_inputs
    for layer in range(sections):
        with jax.named_scope("tower"):
            after = [local, arrived] if layer + 2 == sections else [local]
            layer_weight = loaded(place, section_weights, after)
            near, far = spread_after(local, [layer_weight])
            (local,) = call(
                layer_kernel,
                [((queries, wide), BF16)],
                [place, near, far, layer_weight, *started(place, near, layer_weight)],
            )
            if layer + 1 < sections:
                local = turned(local, "section", 1)
    with jax.named_scope("to_sections"):
        last = sections - 1
        final = jnp.where(section_at == last, local, 0).astype(BF16)
        for other in range(last):
            final = final + lax.ppermute(local, "section", [(last, other)])
    with jax.named_scope("head"):
        head_weight = loaded(place, head_weight, [final])
        near, far = spread_after(final, [head_weight])
        query_cols, slope, pieces = call(
            head_kernel,
            [
                ((queries, wide), BF16),
                ((queries, wide), F32),
                ((cycle, rows, taken + 128), BF16),
            ],
            [place, near, far, head_weight, *started(place, near, head_weight)],
            scratch=[pltpu.VMEM((queries, width), BF16)],
        )
    with jax.named_scope("normed_home"):
        pieces = lax.all_to_all(pieces, "dp", 0, 0)
    with jax.named_scope("score"):
        near, far = spread_after(query_cols, [pieces])
        row_cells, row_positives = query_cells[None, :], positives[None, :]
        group = sections * count * 2
        score, stats, full = call(
            functools.partial(score_kernel, sizes),
            [
                ((cycle * block, queries), F32),
                ((group, 8, queries), F32),
                ((queries, width), BF16),
            ],
            [place, near, far, held, pieces, row_cells, row_positives],
        )
    with jax.named_scope("stats"):
        stats = lax.all_to_all(stats, ("section", "y", "core"), 0, 0)
    with jax.named_scope("grad"):
        part = (sections, count, rows, wide)
        square = ((cycle * block, queries), BF16)
        loss, send, prob, turned_prob = call(
            functools.partial(grad_kernel, sizes),
            [((1, queries), F32), (part, BF16), square, (square[0][::-1], BF16)],
            [place, stats, score, held, pieces, row_cells, row_positives],
        )
        keep, grads = call(
            functools.partial(rest_kernel, sizes),
            [(part, BF16), ((cycle, block, width), BF16)],
            [place, prob, turned_prob, full, held],
        )
    with jax.named_scope("passage_grads"):
        passage_grads = lax.psum_scatter(
            grads.reshape(cycle * block, width), "dp", scatter_dimension=0, tiled=True
        )
    with jax.named_scope("query_grad"):
        keep = (keep.astype(F32) + turned(send, "core", 1).astype(F32)).astype(BF16)
        parts = lax.all_to_all(keep.reshape(sections * count, rows, wide), ("section", "y"), 0, 0)
        (head_grad,) = call(
            head_grad_kernel, [((cycle, rows, wide), BF16)], [place, parts, slope]
        )
        head_grad = lax.all_to_all(head_grad, "dp", 0, 0)
    with jax.named_scope("weight_grad"):
        (part,) = call(
            weight_grad_kernel,
            [((sections, taken // sections, wide), BF16)],
            [place, head_grad, pieces],
        )
        part = lax.all_to_all(part, "section", 0, 0)
        tile = (master.shape, F32)
        new_master, new_moment_one, new_moment_two, passage_grads = call(
            update_kernel,
            [tile, tile, tile, ((block, width), F32)],
            [
                place, part, master, moment_one, moment_two,
                pltpu.with_memory_space_constraint(passage_grads, pltpu.HBM),
            ],
            scratch=[pltpu.VMEM((block, width), BF16), pltpu.SemaphoreType.DMA],
            far_off=(5,),
        )
    return (loss[0], passage_grads, new_master, new_moment_one, new_moment_two)


def solution(mesh):
    sections, cycle, parts = (mesh.shape[axis] for axis in ("section", "dp", "mp"))
    split = Mesh(
        mesh.devices.reshape(sections, cycle, parts // 2, 2), ("section", "dp", "y", "core")
    )
    mp = ("y", "core")
    everything = ("section", "dp") + mp
    tile = P(("section", "dp"), mp)
    return jax.shard_map(
        shards,
        mesh=split,
        in_specs=(
            P("dp", mp),
            P("section", mp),
            P(None, mp),
            P(everything, None),
            P("dp"),
            P(everything),
            P("dp"),
            tile,
            tile,
            tile,
        ),
        out_specs=(P("dp"), P(everything, None), tile, tile, tile),
        check_vma=False,
    )
```
